32 devices in a mesh: dp: 16 (over z, y, x), tensor: 2 (over core).
Axes of the slice: x: 2, y: 2, z: 4, core: 2. Of those that a mesh axis runs over, the one named last changes fastest.
Arguments:
- tokens: bfloat16 [16384, 768], P('dp'), may hold values from -6 to 6
- segments: int32 [16, 1024], P('dp'), may hold values from 0 to 7, never falling along the last dimension, each value on 1 to 512 neighbouring positions
- gain_attn: float32 [768], replicated, may hold values from 0.5 to 1.5
- w_qkv: bfloat16 [768, 3, 768], P(None, None, 'tensor'), may hold values from -0.21875 to 0.21875
- w_attn_out: bfloat16 [768, 768], P('tensor'), may hold values from -1.75 to 1.75
- bias_table: float32 [32, 12], P(None, 'tensor'), may hold values from -4 to 4
- gain_ffn: float32 [768], replicated, may hold values from 0.5 to 1.5
- router: float32 [768, 16], replicated, may hold values from -0.15625 to 0.15625
- expert_in: bfloat16 [16, 768, 3072], P('dp', None, 'tensor'), may hold values from -0.21875 to 0.21875
- expert_out: bfloat16 [16, 3072, 768], P('dp', 'tensor'), may hold values from -4 to 4
- expert_ids: int32 [16384, 1], P('dp'), may hold values from 0 to 15; in each aligned block of 1024 rows (0 to 1023, 1024 to 2047, ...) at most 128 rows name the same one
- cotangent: bfloat16 [16384, 768], P('dp'), may hold values from -21 to 21
Outputs:
- output: bfloat16 [16384, 768], P('dp')
- grad_tokens: float32 [16384, 768], P('dp')
- grad_gain_attn: float32 [768], replicated
- grad_w_qkv: float32 [768, 3, 768], P(None, None, 'tensor')
- grad_w_attn_out: float32 [768, 768], P('tensor')
- grad_bias_table: float32 [32, 12], P(None, 'tensor')
- grad_gain_ffn: float32 [768], replicated
- grad_router: float32 [768, 16], replicated
- grad_expert_in: float32 [16, 768, 3072], P('dp', None, 'tensor')
- grad_expert_out: float32 [16, 3072, 768], P('dp', 'tensor')
The draws below stay inside these ranges and needn't reach their ends.
Inputs may be any that keep to these rules, and one draw needn't show every extreme that they name: `segments`: within each sequence the document numbers never fall, and each document holds at most 512 positions. `expert_ids`: among the 1024 tokens of one sequence no expert is chosen more than 128 times, and some expert is chosen exactly 128 times.
All inputs are finite; a program needn't handle non-finite values.
Results may differ from the reference program's by a relative error of at most 0.013.
The reference program's roundings to bfloat16 on the way count: a program that leaves them out, or rounds other values in their place, can miss the bound.
Values may be sent and summed in bfloat16 or wider, within the bound.
A program may use at most 192 MiB of HBM per device.

```python
import math
import jax
import jax.numpy as jnp
import numpy as np
from jax import lax

D = 768
HEADS = 12
HEAD_DIM = 64
FF = 3072
NB = 32
LENGTH = 1024
DOCS = 8
EXPERTS = 16
SEQS = 16
TOKENS = 16384
CAP = 128


def draw_cotangent(key, part):
    key = jax.random.fold_in(key, 5)
    normal_key = jax.random.fold_in(key, 0)
    rising = 1.0 + 2.0 * jnp.arange(TOKENS, dtype=jnp.float32)[:, None] / TOKENS
    base_draw = jnp.clip(jax.random.normal(normal_key, (TOKENS, D), jnp.float32), -6.0, 6.0)
    return (base_draw * rising).astype(jnp.bfloat16)


def block_scale(rng, shape, shards, smallest, high):
    loudness = 1.0
    for dim, shards_of in shards:
        heights = jax.random.uniform(jax.random.fold_in(jax.random.fold_in(rng, 6), dim), (shards_of,), jnp.float32, smallest / len(shards), high / len(shards))
        loudness = loudness * jnp.repeat(jnp.exp(heights), shape[dim] // shards_of).reshape((-1,) + (1,) * (len(shape) - 1 - dim))
    return loudness


def length_profile(number_of, total, reach, slope):
    portions = [(1 << 20) // math.isqrt(standing ** slope) + 1 for standing in range(2, number_of + 1)]
    surplus, counts = total - reach - (number_of - 1), [1] * (number_of - 1)
    while surplus > 0:
        free = [i for i in range(number_of - 1) if counts[i] < reach]
        pool, budget = sum([portions[i] for i in free]), surplus
        for i in free:
            extra = min(reach - counts[i], max(1, budget * portions[i] // pool), surplus)
            counts[i] = counts[i] + extra
            surplus = surplus - extra
    return np.array([reach] + counts)


def uneven(stream_key, amount, total, bound, skew):
    if amount == 2:
        one = jax.random.randint(stream_key, (), max(1, total - bound), min(bound, total - 1) + 1)
        return jnp.stack([one, total - one])
    sizes = jnp.asarray(length_profile(amount, total, bound, skew), jnp.int32)
    twos = (amount - 1) // 2
    donor, receiver = sizes[1:1 + 2 * twos:2], sizes[2:2 + 2 * twos:2]
    slack = jnp.minimum(donor - 1, bound - receiver)
    passed = jax.random.randint(jax.random.fold_in(stream_key, 1), (twos,), 0, 1 << 20) % (slack + 1)
    sizes = sizes.at[1:1 + 2 * twos:2].set(donor - passed).at[2:2 + 2 * twos:2].set(receiver + passed)
    return sizes[jax.random.permutation(jax.random.fold_in(stream_key, 2), amount)]


def deal_out(own_key, own, number, rows, number_of, top, limit, lean):
    order = jax.random.permutation(own_key, number_of)
    crowded, usual = shares(number_of, rows * top, limit, lean, True), shares(number_of, rows * top, limit, lean, False)
    places = jnp.arange(number_of)

    def named(lengths, rotation):
        used = int((lengths > 0).sum())
        fixed = max(1, used // 4)
        moved = fixed + (places - fixed + rotation * (used - fixed)) % max(1, number_of - fixed)
        return jnp.zeros((number_of,), jnp.int32).at[order[jnp.where(places < fixed, places, moved)]].set(jnp.asarray(lengths, jnp.int32))

    lengths = jnp.where(number % 4 == 0, named(crowded, number // 4), named(usual, number - number // 4 - 1))
    mixed = jax.random.permutation(jax.random.fold_in(own, 3), number_of)
    source_of, taker = mixed[0:number_of // 2 * 2:2], mixed[1:number_of // 2 * 2:2]
    slack = jnp.minimum(lengths[source_of] - 1, limit - lengths[taker]) // 2
    slack = jnp.where((source_of == order[0]) | (taker == order[0]) | (lengths[taker] == 0), 0, jnp.maximum(slack, 0))
    moved = jax.random.randint(jax.random.fold_in(own, 4), (number_of // 2,), 0, 1 << 20) % (slack + 1)
    lengths = lengths.at[source_of].add(-moved).at[taker].add(moved)
    items = jnp.searchsorted(jnp.cumsum(lengths), jnp.arange(rows * top), side="right").astype(jnp.int32)
    grid = items.reshape(top, rows).T
    grid = grid[jax.random.permutation(jax.random.fold_in(own, 1), rows)]
    rotation = jax.random.randint(jax.random.fold_in(own, 2), (rows, 1), 0, top)
    return jnp.take_along_axis(grid, (jnp.arange(top)[None, :] + rotation) % top, axis=1)


def shares(amount, total, most, slope, full):
    loads = [(1 << 20) // math.isqrt(rank ** slope) + 1 for rank in range(1, amount + 1)]
    largest = most if full else min(most, max(-(-total // amount), total * loads[0] // sum(loads)))
    least = 1 if total - largest >= amount - 1 else 0
    counts, rest = [largest] + [least] * (amount - 1), total - largest - least * (amount - 1)
    while rest > 0:
        free = [i for i in range(1, amount) if counts[i] < largest] or [i for i in range(1, amount) if counts[i] < most]
        whole, left = sum([loads[i] for i in free]), rest
        for i in free:
            addition = min(most - counts[i], max(1, left * loads[i] // whole), rest)
            counts[i] = counts[i] + addition
            rest = rest - addition
    return np.array(counts)


def noise(own_key, dims, deviation, reach, shards=(), kind=jnp.bfloat16):
    level = block_scale(own_key, dims, shards, -0.22, 0.18) if shards else 1.0
    drawn = jax.random.normal(own_key, dims, jnp.float32) * deviation * level
    return jnp.minimum(jnp.maximum(drawn, -reach), reach).astype(kind)


def setup_inputs(seed: int = 0) -> dict:
    key_list = jax.random.split(jax.random.key(seed), 13)
    tokens = noise(key_list[0], (TOKENS, D), 1.0, 6.0, ((0, 16),))
    segments = jax.vmap(lambda own: jnp.searchsorted(jnp.cumsum(uneven(own, DOCS, LENGTH, LENGTH // 2, 1)), jnp.arange(LENGTH), side="right"))(jax.random.split(key_list[1], SEQS)).reshape((SEQS, LENGTH)).astype(jnp.int32)
    gain_attn = jnp.clip(1.0 + 0.1 * jax.random.normal(key_list[2], (D,), jnp.float32), 0.5, 1.5)
    w_qkv = noise(key_list[3], (D, 3, D), D ** -0.5, 0.21875, ((2, 2),))
    w_attn_out = noise(key_list[4], (D, D), (D // 64) ** -0.5, 1.75, ((0, 2),))
    bias_table = noise(key_list[5], (NB, HEADS), 1.0, 4.0, ((1, 2),), jnp.float32)
    gain_ffn = jnp.clip(1.0 + 0.1 * jax.random.normal(key_list[6], (D,), jnp.float32), 0.5, 1.5)
    router = noise(key_list[7], (D, EXPERTS), (2 * D) ** -0.5, 0.15625, (), jnp.float32)
    expert_in = noise(key_list[8], (EXPERTS, D, FF), D ** -0.5, 0.21875, ((0, 16), (2, 2)))
    expert_out = noise(key_list[9], (EXPERTS, FF, D), (EXPERTS * FF ** -0.5), 4.0, ((0, 16), (1, 2)))
    expert_ids_keys = jax.random.split(jax.random.fold_in(key_list[10], 1), TOKENS // LENGTH)
    expert_ids_turns = jax.random.permutation(jax.random.fold_in(key_list[10], 3), TOKENS // LENGTH)
    expert_ids = jax.vmap(lambda own, number: deal_out(jax.random.fold_in(key_list[10], 2), own, number, LENGTH, EXPERTS, 1, CAP, 2))(expert_ids_keys, expert_ids_turns).reshape((TOKENS, 1))
    cotangent = draw_cotangent(jax.random.fold_in(key_list[12], 71), 0)
    return {"tokens": tokens, "segments": segments, "gain_attn": gain_attn, "w_qkv": w_qkv, "w_attn_out": w_attn_out, "bias_table": bias_table, "gain_ffn": gain_ffn, "router": router, "expert_in": expert_in, "expert_out": expert_out, "expert_ids": expert_ids, "cotangent": cotangent}


epsilon = 1e-06
highest = lax.Precision.HIGHEST
bucket_edges = (8, 12, 16, 23, 32, 46, 64, 91)

@jax.custom_vjp
def low(v):
    return lax.optimization_barrier(v.astype(jnp.bfloat16)).astype(jnp.float32)

@jax.custom_vjp
def low_back(v):
    return v

def low_keep(v):
    return (low(v), None)

def low_pass(kept, grad):
    return (grad,)

def back_keep(v):
    return (v, None)

def back_low(kept, grad):
    return (low(grad),)
low.defvjp(low_keep, low_pass)
low_back.defvjp(back_keep, back_low)

def bucket_ids(row_positions, col_positions):
    offset = col_positions[None, :] - row_positions[:, None]
    distance = jnp.abs(offset)
    far_part = jnp.zeros_like(distance)
    for edge_value in bucket_edges:
        far_part = far_part + (distance >= edge_value).astype(jnp.int32)
    near_far = jnp.where(distance < 8, distance, 7 + far_part)
    return near_far + NB // 2 * (offset > 0).astype(jnp.int32)

def rms_scale(values, gain_vec):
    return values * lax.rsqrt(lax.optimization_barrier(jnp.mean(values * values, axis=-1, keepdims=True)) + epsilon) * gain_vec

def attend_one(queries, keys_all, values_all, seg_row, table_t):
    block_rows = min(512, LENGTH)
    col_positions = jnp.arange(LENGTH, dtype=jnp.int32)

    def one_block(block_index):
        row_start = block_index * block_rows
        row_positions = row_start + jnp.arange(block_rows, dtype=jnp.int32)
        query_block = lax.dynamic_slice_in_dim(queries, row_start, block_rows, 0)
        seg_block = lax.dynamic_slice_in_dim(seg_row, row_start, block_rows, 0)
        raw_scores = low_back(jnp.einsum('qhd,khd->hqk', query_block, keys_all, precision=highest) * 0.125)
        biases = jnp.take(table_t, bucket_ids(row_positions, col_positions), axis=1)
        same_doc = seg_block[:, None] == seg_row[None, :]
        scores = jnp.where(same_doc[None], raw_scores + biases, -1e+30)
        row_peak = lax.optimization_barrier(jnp.max(scores, axis=-1, keepdims=True))
        shifted = jnp.exp(scores - row_peak)
        weights = shifted / lax.optimization_barrier(jnp.sum(shifted, axis=-1, keepdims=True))
        return jnp.einsum('hqk,khd->qhd', low(weights), values_all, precision=highest)
    blocks_out = lax.map(jax.checkpoint(one_block), jnp.arange(LENGTH // block_rows, dtype=jnp.int32))
    return blocks_out.reshape(LENGTH, HEADS, HEAD_DIM)

def reference(tokens, segments, gain_attn, w_qkv, w_attn_out, bias_table, gain_ffn, router, expert_in, expert_out, expert_ids, cotangent):
    chosen = expert_ids[:, 0]
    one_hot = (chosen[:, None] == jnp.arange(EXPERTS, dtype=jnp.int32)[None, :]).astype(jnp.int32)
    per_seq = one_hot.reshape(SEQS, LENGTH, EXPERTS)
    ranks = jnp.cumsum(per_seq, axis=1) - per_seq
    slot_ids = lax.optimization_barrier(jnp.sum(ranks * per_seq, axis=2)).reshape(TOKENS)
    seq_ids = jnp.arange(TOKENS, dtype=jnp.int32) // LENGTH
    target_rows = chosen * (SEQS * CAP) + seq_ids * CAP + slot_ids
    one_hot_float = one_hot.astype(jnp.float32)

    def layer(inputs32, gain_one, attn_weight, proj_weight, table, gain_two, router_weight, weight_in, weight_out):
        normed = low(rms_scale(inputs32, gain_one))
        packed = low_back(low(jnp.dot(normed, attn_weight.reshape(D, 3 * D), precision=highest)))
        packed = packed.reshape(SEQS, LENGTH, 3, HEADS, HEAD_DIM)
        table_t = table.T

        def per_sequence(members):
            seq_packed, seg_row = members
            return attend_one(seq_packed[:, 0], seq_packed[:, 1], seq_packed[:, 2], seg_row, table_t)
        attended = lax.map(per_sequence, (packed, segments))
        mixed_heads = low_back(low(attended.reshape(TOKENS, D)))
        attn_out = low_back(jnp.dot(mixed_heads, proj_weight, precision=highest))
        hidden = inputs32 + attn_out
        ffn_in = rms_scale(hidden, gain_two)
        router_logits = jnp.dot(ffn_in, router_weight, precision=highest)
        logit_peak = lax.optimization_barrier(jnp.max(router_logits, axis=1, keepdims=True))
        router_exp = jnp.exp(router_logits - logit_peak)
        router_probs = router_exp / lax.optimization_barrier(jnp.sum(router_exp, axis=1, keepdims=True))
        gate_prob = lax.optimization_barrier(jnp.sum(router_probs * one_hot_float, axis=1))
        sent_rows = low_back(low(ffn_in))
        dispatched = jnp.zeros((EXPERTS * SEQS * CAP, D), jnp.float32).at[target_rows].set(sent_rows)

        def per_expert(members):
            rows_in, matrix_in, matrix_out = members
            inner_act = low_back(jnp.dot(rows_in, matrix_in, precision=highest))
            return jnp.dot(low(jax.nn.gelu(inner_act, approximate=True)), matrix_out, precision=highest)
        returned = lax.map(jax.checkpoint(per_expert), (dispatched.reshape(EXPERTS, SEQS * CAP, D), weight_in, weight_out))
        returned = low_back(low(returned)).reshape(EXPERTS * SEQS * CAP, D)
        return hidden + gate_prob[:, None] * returned[target_rows]
    operands = (tokens.astype(jnp.float32), gain_attn, w_qkv.astype(jnp.float32), w_attn_out.astype(jnp.float32), bias_table, gain_ffn, router, expert_in.astype(jnp.float32), expert_out.astype(jnp.float32))
    result, pull_back = jax.vjp(layer, *operands)
    gradients = pull_back(cotangent.astype(jnp.float32))
    return (result.astype(jnp.bfloat16), gradients[0], gradients[1], gradients[2], gradients[3], gradients[4], gradients[5], gradients[6], gradients[7], gradients[8])
```

```python
import jax
import jax.numpy as jnp
from jax import lax
from jax.experimental import pallas as pl
from jax.experimental.pallas import tpu as pltpu
from jax.sharding import PartitionSpec as P

epsilon = 1e-06
highest = lax.Precision.HIGHEST
bucket_edges = (8, 12, 16, 23, 32, 46, 64, 91)


def bucket_ids(row_positions, col_positions, half_count):
    offset = col_positions[None, :] - row_positions[:, None]
    distance = jnp.abs(offset)
    far_part = jnp.zeros_like(distance)
    for edge_value in bucket_edges:
        far_part = far_part + (distance >= edge_value).astype(jnp.int32)
    near_far = jnp.where(distance < 8, distance, 7 + far_part)
    return near_far + half_count * (offset > 0).astype(jnp.int32)


NEAR = 128
ROWS = 256
SPAN = ROWS + 2 * NEAR


def near_buckets(bucket_count):
    zero = jnp.zeros((1,), jnp.int32)
    relative = jnp.arange(SPAN, dtype=jnp.int32) - NEAR
    return bucket_ids(zero, relative, bucket_count // 2)[0]


def skew(values, right):
    rows = lax.broadcasted_iota(jnp.int32, values.shape, 0)
    width = values.shape[1]
    step = 1
    while step < values.shape[0]:
        rolled = pltpu.roll(values, step if right else width - step, 1)
        values = jnp.where((rows & step) != 0, rolled, values)
        step *= 2
    return values


def fill_strip(strip, vec_ref, length):
    left = length - ROWS - NEAR
    for head in range(2):
        row = vec_ref[0, head : head + 1, :]
        low = row[:, :1]
        high = row[:, SPAN - 1 :]
        spread = skew(jnp.broadcast_to(row, (ROWS, SPAN)), True)
        lanes = lax.broadcasted_iota(jnp.int32, (ROWS, SPAN), 1)
        rows = lax.broadcasted_iota(jnp.int32, (ROWS, SPAN), 0)
        strip[head, :, left : left + SPAN] = jnp.where(lanes < rows, low, spread)
        strip[head, :, :left] = jnp.broadcast_to(low, (ROWS, left))
        rest = strip.shape[2] - left - SPAN
        strip[head, :, left + SPAN :] = jnp.broadcast_to(high, (ROWS, rest))


def head_lanes(values, head):
    lanes = lax.broadcasted_iota(jnp.int32, values.shape, 1)
    keep = (lanes < 64) if head == 0 else (lanes >= 64)
    return jnp.where(keep, values, jnp.zeros_like(values))


def dot_nt(left, right):
    return lax.dot_general(left, right, (((1,), (1,)), ((), ())), preferred_element_type=jnp.float32)


def dot_tn(left, right):
    return lax.dot_general(left, right, (((0,), (0,)), ((), ())), preferred_element_type=jnp.float32)


def dot_nn(left, right):
    return jnp.dot(left, right, preferred_element_type=jnp.float32)


def forward_kernel(q_ref, k_ref, v_ref, seg_col, seg_row, vec_ref, out_ref, lse_ref, strip):
    length = k_ref.shape[0]
    block = pl.program_id(1)

    @pl.when(block == 0)
    def _():
        fill_strip(strip, vec_ref, length)

    start = pl.multiple_of(length - ROWS - block * ROWS, ROWS)
    same_doc = seg_col[...] == seg_row[...]
    outs = []
    norms = []
    for head in range(2):
        scores = dot_nt(head_lanes(q_ref[...], head), k_ref[...]) * 0.125
        scores = scores + strip[head, :, pl.ds(start, length)]
        scores = jnp.where(same_doc, scores, -1e30)
        peak = jnp.max(scores, axis=1, keepdims=True)
        shifted = jnp.exp(scores - peak)
        total = jnp.sum(shifted, axis=1, keepdims=True)
        weights = (shifted * (1.0 / total)).astype(jnp.bfloat16)
        outs.append(dot_nn(weights, v_ref[...]))
        norms.append(peak + jnp.log(total))
    lanes = lax.broadcasted_iota(jnp.int32, out_ref.shape, 1)
    out_ref[...] = jnp.where(lanes < 64, outs[0], outs[1]).astype(jnp.bfloat16)
    lse_ref[...] = jnp.where(lanes < 64, norms[0], norms[1])


def backward_kernel(
    q_ref, k_ref, v_ref, g_ref, seg_col, seg_row, vec_ref, lse_ref,
    dq_ref, dk_ref, dv_ref, diag_ref, far_ref, strip, sums, dk_sum, dv_sum,
):
    length = k_ref.shape[0]
    block = pl.program_id(1)
    left = length - ROWS - NEAR

    @pl.when(block == 0)
    def _():
        fill_strip(strip, vec_ref, length)
        sums[...] = jnp.zeros_like(sums)
        dk_sum[...] = jnp.zeros_like(dk_sum)
        dv_sum[...] = jnp.zeros_like(dv_sum)

    start = pl.multiple_of(length - ROWS - block * ROWS, ROWS)
    same_doc = seg_col[...] == seg_row[...]
    queries_grad = []
    for head in range(2):
        query = head_lanes(q_ref[...], head)
        out_grad = head_lanes(g_ref[...], head)
        scores = dot_nt(query, k_ref[...]) * 0.125
        scores = scores + strip[head, :, pl.ds(start, length)]
        norm = lse_ref[:, 64 * head : 64 * head + 1]
        probs = jnp.where(same_doc, jnp.exp(scores - norm), 0.0)
        grad_probs = dot_nt(out_grad, v_ref[...])
        row_dot = jnp.sum(probs * grad_probs, axis=1, keepdims=True)
        grad_scores = probs * (grad_probs - row_dot)
        sums[head, :, pl.ds(start, length)] += grad_scores
        low_scores = grad_scores.astype(jnp.bfloat16)
        queries_grad.append(dot_nn(low_scores, k_ref[...]))
        dk_sum[...] += dot_tn(low_scores, query)
        dv_sum[...] += dot_tn(probs.astype(jnp.bfloat16), out_grad)
    lanes = lax.broadcasted_iota(jnp.int32, dq_ref.shape, 1)
    joined = jnp.where(lanes < 64, queries_grad[0], queries_grad[1]) * 0.125
    dq_ref[...] = joined.astype(jnp.bfloat16)

    @pl.when(block == pl.num_programs(1) - 1)
    def _():
        dk_ref[...] = (dk_sum[...] * 0.125).astype(jnp.bfloat16)
        dv_ref[...] = dv_sum[...].astype(jnp.bfloat16)
        for head in range(2):
            near = sums[head, :, left : left + SPAN]
            lanes = lax.broadcasted_iota(jnp.int32, near.shape, 1)
            rows = lax.broadcasted_iota(jnp.int32, near.shape, 0)
            relative = lanes - rows - NEAR
            low = jnp.sum(jnp.where(relative <= -NEAR, near, 0.0), axis=0, keepdims=True)
            high = jnp.sum(jnp.where(relative >= NEAR, near, 0.0), axis=0, keepdims=True)
            inside = jnp.where(jnp.abs(relative) < NEAR, near, 0.0)
            diag_ref[0, head : head + 1, :] = jnp.sum(skew(inside, False), axis=0, keepdims=True)
            low_total = jnp.sum(low) + jnp.sum(sums[head, :, :left])
            high_total = jnp.sum(high) + jnp.sum(sums[head, :, left + SPAN :])
            side = lax.broadcasted_iota(jnp.int32, (1, 128), 1)
            far_ref[0, head : head + 1, :] = jnp.where(side < 64, low_total, high_total)


def attention_specs(length, pairs):
    whole = lambda part: pl.BlockSpec((length, 128), lambda p, b: (0, part * pairs + p))
    rows = pl.BlockSpec((ROWS, 128), lambda p, b: (b, p))
    seg_col = pl.BlockSpec((ROWS, 1), lambda p, b: (b, 0))
    seg_row = pl.BlockSpec((1, length), lambda p, b: (0, 0))
    vec = pl.BlockSpec((1, 2, SPAN), lambda p, b: (p, 0, 0))
    return whole, rows, seg_col, seg_row, vec


def attention_forward(packed, segment_row, bias_vec):
    length = packed.shape[0]
    pairs = packed.shape[1] // (3 * 128)
    whole, rows, seg_col, seg_row, vec = attention_specs(length, pairs)
    return pl.pallas_call(
        forward_kernel,
        grid=(pairs, length // ROWS),
        in_specs=[rows, whole(1), whole(2), seg_col, seg_row, vec],
        out_specs=[rows, rows],
        out_shape=[
            jax.ShapeDtypeStruct((length, pairs * 128), jnp.bfloat16),
            jax.ShapeDtypeStruct((length, pairs * 128), jnp.float32),
        ],
        scratch_shapes=[pltpu.VMEM((2, ROWS, 2 * length - ROWS), jnp.float32)],
        compiler_params=pltpu.CompilerParams(vmem_limit_bytes=40 * 1024 * 1024),
        name="attention_forward",
    )(packed, packed, packed, segment_row[:, None], segment_row[None, :], bias_vec)


def attention_backward(packed, out_grad, segment_row, bias_vec, log_norm):
    length = packed.shape[0]
    pairs = packed.shape[1] // (3 * 128)
    whole, rows, seg_col, seg_row, vec = attention_specs(length, pairs)
    low = jax.ShapeDtypeStruct((length, pairs * 128), jnp.bfloat16)
    return pl.pallas_call(
        backward_kernel,
        grid=(pairs, length // ROWS),
        in_specs=[rows, whole(1), whole(2), rows, seg_col, seg_row, vec, rows],
        out_specs=[
            rows,
            whole(0),
            whole(0),
            vec,
            pl.BlockSpec((1, 2, 128), lambda p, b: (p, 0, 0)),
        ],
        out_shape=[
            low,
            low,
            low,
            jax.ShapeDtypeStruct((pairs, 2, SPAN), jnp.float32),
            jax.ShapeDtypeStruct((pairs, 2, 128), jnp.float32),
        ],
        scratch_shapes=[
            pltpu.VMEM((2, ROWS, 2 * length - ROWS), jnp.float32),
            pltpu.VMEM((2, ROWS, 2 * length - ROWS), jnp.float32),
            pltpu.VMEM((length, 128), jnp.float32),
            pltpu.VMEM((length, 128), jnp.float32),
        ],
        compiler_params=pltpu.CompilerParams(vmem_limit_bytes=48 * 1024 * 1024),
        name="attention_backward",
    )(packed, packed, packed, out_grad, segment_row[:, None], segment_row[None, :], bias_vec, log_norm)


def gelu_tanh(inner_act):
    return jax.nn.gelu(inner_act, approximate=True)


def swap(values):
    return lax.ppermute(values, "tensor", [(0, 1), (1, 0)])


def heads_total(partial_sum):
    return partial_sum + swap(partial_sum)


def exchange(rows, model_width):
    grouped = rows.reshape(lax.axis_size("dp"), -1, model_width)
    return lax.all_to_all(grouped, "dp", split_axis=0, concat_axis=0, tiled=True)


def to_owners(rows, model_width):
    arrived = exchange(rows, model_width)
    return jnp.concatenate([arrived, swap(arrived)], axis=0)


def to_senders(partial_rows, model_width):
    kept, given = jnp.split(partial_rows.reshape(2, -1, model_width), 2, axis=0)
    summed = kept + swap(given.astype(jnp.bfloat16)).astype(jnp.float32)
    arrived = exchange(summed.astype(jnp.bfloat16), model_width).reshape(-1, model_width)
    return jnp.concatenate([arrived, swap(arrived)], axis=0)


def per_device(
    tokens,
    segments,
    gain_attn,
    w_qkv,
    w_attn_out,
    bias_table,
    gain_ffn,
    router,
    expert_in,
    expert_out,
    expert_ids,
    cotangent,
):
    length, model_width = tokens.shape
    head_cols = w_qkv.shape[2]
    heads_here = bias_table.shape[1]
    head_size = head_cols // heads_here
    experts_all = router.shape[1]
    experts_here = expert_in.shape[0]
    capacity = max(2, 2 * length // experts_all)
    half = capacity // 2
    segment_row = segments[0]
    bucket_count = bias_table.shape[0]
    near_hot = (
        near_buckets(bucket_count)[:, None] == jnp.arange(bucket_count, dtype=jnp.int32)[None, :]
    ).astype(jnp.float32)
    bias_vec = jnp.sum(near_hot[None] * bias_table.T[:, None, :], axis=2)
    bias_vec = bias_vec.reshape(heads_here // 2, 2, SPAN)
    inputs32 = tokens.astype(jnp.float32)
    scale_one = lax.rsqrt(jnp.mean(inputs32 * inputs32, axis=1, keepdims=True) + epsilon)
    normed_one = inputs32 * scale_one
    normed = (normed_one * gain_attn).astype(jnp.bfloat16)
    w_flat = w_qkv.reshape(model_width, 3 * head_cols)
    packed = jnp.dot(normed, w_flat, preferred_element_type=jnp.float32).astype(jnp.bfloat16)
    mixed_heads, log_norm = attention_forward(packed, segment_row, bias_vec)
    attn_part = jnp.dot(mixed_heads, w_attn_out, preferred_element_type=jnp.float32)
    hidden = inputs32 + heads_total(attn_part)
    scale_two = lax.rsqrt(jnp.mean(hidden * hidden, axis=1, keepdims=True) + epsilon)
    normed_two = hidden * scale_two
    ffn_in = normed_two * gain_ffn
    router_logits = jnp.dot(ffn_in, router, precision=highest)
    logit_peak = jnp.max(router_logits, axis=1, keepdims=True)
    router_exp = jnp.exp(router_logits - logit_peak)
    router_probs = router_exp / jnp.sum(router_exp, axis=1, keepdims=True)
    chosen = expert_ids[:, 0]
    one_hot_int = (chosen[:, None] == jnp.arange(experts_all, dtype=jnp.int32)[None, :]).astype(
        jnp.int32
    )
    one_hot_float = one_hot_int.astype(jnp.float32)
    gate_prob = jnp.sum(router_probs * one_hot_float, axis=1)
    earlier = jnp.arange(length)[None, :] < jnp.arange(length)[:, None]
    ranks = jnp.dot(
        earlier.astype(jnp.bfloat16),
        one_hot_float.astype(jnp.bfloat16),
        preferred_element_type=jnp.float32,
    )
    slot_ids = jnp.sum(ranks * one_hot_float, axis=1).astype(jnp.int32)
    side = (slot_ids >= half).astype(jnp.int32)
    other_side = (side != lax.axis_index("tensor")).astype(jnp.int32)
    target_rows = chosen * half + slot_ids - side * half + other_side * (experts_all * half)
    own_slots = jnp.arange(experts_all * half, dtype=jnp.int32)
    place = (own_slots[:, None] == target_rows[None, :]).astype(jnp.bfloat16)
    all_slots = jnp.arange(2 * experts_all * half, dtype=jnp.int32)
    pick = (target_rows[:, None] == all_slots[None, :]).astype(jnp.bfloat16)
    send_rows = jnp.dot(place, ffn_in.astype(jnp.bfloat16), preferred_element_type=jnp.float32)
    expert_rows = to_owners(send_rows.astype(jnp.bfloat16), model_width).reshape(
        -1, experts_here, half, model_width
    )
    upstream = cotangent.astype(jnp.float32)
    back_rows = (gate_prob[:, None] * upstream).astype(jnp.bfloat16)
    back_sent = jnp.dot(place, back_rows, preferred_element_type=jnp.float32)
    expert_grads = to_owners(back_sent.astype(jnp.bfloat16), model_width).reshape(
        -1, experts_here, half, model_width
    )
    inner_act = jnp.einsum(
        "secd,edf->secf", expert_rows, expert_in, preferred_element_type=jnp.float32
    )
    activated, gelu_back = jax.vjp(gelu_tanh, inner_act)
    act_low = activated.astype(jnp.bfloat16)
    expert_part = jnp.einsum(
        "secf,efd->secd", act_low, expert_out, preferred_element_type=jnp.float32
    )
    returned = to_senders(expert_part, model_width)
    picked = jnp.dot(pick, returned, preferred_element_type=jnp.float32)
    output = (hidden + gate_prob[:, None] * picked).astype(jnp.bfloat16)
    grad_gate = jnp.sum(upstream * picked, axis=1)
    grad_act = jnp.einsum(
        "secd,efd->secf", expert_grads, expert_out, preferred_element_type=jnp.float32
    )
    grad_inner = gelu_back(grad_act)[0].astype(jnp.bfloat16)
    grad_expert_out = jnp.einsum(
        "secf,secd->efd", act_low, expert_grads, preferred_element_type=jnp.float32
    )
    grad_expert_in = jnp.einsum(
        "secd,secf->edf", expert_rows, grad_inner, preferred_element_type=jnp.float32
    )
    grad_rows = jnp.einsum(
        "secf,edf->secd", grad_inner, expert_in, preferred_element_type=jnp.float32
    )
    grad_sent = jnp.dot(
        pick, to_senders(grad_rows, model_width), preferred_element_type=jnp.float32
    )
    grad_logits = router_probs * (one_hot_float - gate_prob[:, None]) * grad_gate[:, None]
    grad_router = jnp.dot(ffn_in.T, grad_logits, precision=highest)
    grad_ffn_in = grad_sent + jnp.dot(grad_logits, router.T, precision=highest)
    grad_gain_ffn = jnp.sum(grad_ffn_in * normed_two, axis=0)
    grad_norm_two = grad_ffn_in * gain_ffn
    grad_hidden = upstream + scale_two * (
        grad_norm_two - normed_two * jnp.mean(grad_norm_two * normed_two, axis=1, keepdims=True)
    )
    grad_attn = grad_hidden.astype(jnp.bfloat16)
    grad_w_attn_out = jnp.dot(mixed_heads.T, grad_attn, preferred_element_type=jnp.float32)
    grad_mixed = jnp.dot(grad_attn, w_attn_out.T, preferred_element_type=jnp.float32).astype(
        jnp.bfloat16
    )
    early = lax.psum(
        (grad_w_attn_out.astype(jnp.bfloat16), grad_gain_ffn, grad_router), "dp"
    )
    grad_queries, grad_keys, grad_values, diagonals, far = attention_backward(
        packed, grad_mixed, segment_row, bias_vec, log_norm
    )
    grad_table = jnp.sum(diagonals.reshape(heads_here, SPAN)[:, :, None] * near_hot[None], axis=1)
    far = far.reshape(heads_here, 128)
    half_count = bucket_count // 2
    bucket_row = jnp.arange(bucket_count, dtype=jnp.int32)[None, :]
    grad_table = grad_table + jnp.where(bucket_row == half_count - 1, far[:, :1], 0.0)
    grad_table = grad_table + jnp.where(bucket_row == bucket_count - 1, far[:, 127:], 0.0)
    grad_packed = jnp.concatenate([grad_queries, grad_keys, grad_values], axis=1)
    grad_packed, early = lax.optimization_barrier((grad_packed, early))
    grad_w_qkv = jnp.dot(normed.T, grad_packed, preferred_element_type=jnp.float32).reshape(
        model_width, 3, head_cols
    )
    grad_normed = heads_total(jnp.dot(grad_packed, w_flat.T, preferred_element_type=jnp.float32))
    grad_gain_attn = jnp.sum(grad_normed * normed_one, axis=0)
    grad_norm_one = grad_normed * gain_attn
    grad_tokens = grad_hidden + scale_one * (
        grad_norm_one - normed_one * jnp.mean(grad_norm_one * normed_one, axis=1, keepdims=True)
    )
    total_w_qkv = lax.psum(grad_w_qkv.astype(jnp.bfloat16), "dp")
    total_gain, total_table = lax.psum((grad_gain_attn, grad_table.T), "dp")
    return (
        output,
        grad_tokens,
        total_gain,
        total_w_qkv.astype(jnp.float32),
        early[0].astype(jnp.float32),
        total_table,
        early[1],
        early[2],
        grad_expert_in,
        grad_expert_out,
    )


def solution(mesh):
    return jax.shard_map(
        per_device,
        mesh=mesh,
        in_specs=(
            P("dp", None),
            P("dp", None),
            P(),
            P(None, None, "tensor"),
            P("tensor", None),
            P(None, "tensor"),
            P(),
            P(),
            P("dp", None, "tensor"),
            P("dp", "tensor", None),
            P("dp", None),
            P("dp", None),
        ),
        out_specs=(
            P("dp", None),
            P("dp", None),
            P(),
            P(None, None, "tensor"),
            P("tensor", None),
            P(None, "tensor"),
            P(),
            P(),
            P("dp", None, "tensor"),
            P("dp", "tensor", None),
        ),
        check_vma=False,
    )
```

```python
import jax
import jax.numpy as jnp
from jax import lax
from jax.experimental import pallas as pl
from jax.experimental.pallas import tpu as pltpu
from jax.sharding import PartitionSpec as P

epsilon = 1e-06
highest = lax.Precision.HIGHEST
bucket_edges = (8, 12, 16, 23, 32, 46, 64, 91)


def bucket_ids(row_positions, col_positions, half_count):
    offset = col_positions[None, :] - row_positions[:, None]
    distance = jnp.abs(offset)
    far_part = jnp.zeros_like(distance)
    for edge_value in bucket_edges:
        far_part = far_part + (distance >= edge_value).astype(jnp.int32)
    near_far = jnp.where(distance < 8, distance, 7 + far_part)
    return near_far + half_count * (offset > 0).astype(jnp.int32)


NEAR = 128
ROWS = 256
SPAN = ROWS + 2 * NEAR


def near_buckets(bucket_count):
    zero = jnp.zeros((1,), jnp.int32)
    relative = jnp.arange(SPAN, dtype=jnp.int32) - NEAR
    return bucket_ids(zero, relative, bucket_count // 2)[0]


def skew(values, right):
    rows = lax.broadcasted_iota(jnp.int32, values.shape, 0)
    width = values.shape[1]
    step = 1
    while step < values.shape[0]:
        rolled = pltpu.roll(values, step if right else width - step, 1)
        values = jnp.where((rows & step) != 0, rolled, values)
        step *= 2
    return values


def fill_strip(strip, vec_ref, length):
    left = length - ROWS - NEAR
    for head in range(2):
        row = vec_ref[0, head : head + 1, :]
        low = row[:, :1]
        high = row[:, SPAN - 1 :]
        spread = skew(jnp.broadcast_to(row, (ROWS, SPAN)), True)
        lanes = lax.broadcasted_iota(jnp.int32, (ROWS, SPAN), 1)
        rows = lax.broadcasted_iota(jnp.int32, (ROWS, SPAN), 0)
        strip[head, :, left : left + SPAN] = jnp.where(lanes < rows, low, spread)
        strip[head, :, :left] = jnp.broadcast_to(low, (ROWS, left))
        rest = strip.shape[2] - left - SPAN
        strip[head, :, left + SPAN :] = jnp.broadcast_to(high, (ROWS, rest))


def head_lanes(values, head):
    lanes = lax.broadcasted_iota(jnp.int32, values.shape, 1)
    keep = (lanes < 64) if head == 0 else (lanes >= 64)
    return jnp.where(keep, values, jnp.zeros_like(values))


def dot_nt(left, right):
    return lax.dot_general(left, right, (((1,), (1,)), ((), ())), preferred_element_type=jnp.float32)


def dot_tn(left, right):
    return lax.dot_general(left, right, (((0,), (0,)), ((), ())), preferred_element_type=jnp.float32)


def dot_nn(left, right):
    return jnp.dot(left, right, preferred_element_type=jnp.float32)


def forward_kernel(q_ref, k_ref, v_ref, seg_col, seg_row, vec_ref, out_ref, lse_ref, strip):
    length = k_ref.shape[0]
    block = pl.program_id(1)

    @pl.when(block == 0)
    def _():
        fill_strip(strip, vec_ref, length)

    start = pl.multiple_of(length - ROWS - block * ROWS, ROWS)
    same_doc = seg_col[...] == seg_row[...]
    outs = []
    norms = []
    for head in range(2):
        scores = dot_nt(head_lanes(q_ref[...], head), k_ref[...]) * 0.125
        scores = scores + strip[head, :, pl.ds(start, length)]
        scores = jnp.where(same_doc, scores, -1e30)
        peak = jnp.max(scores, axis=1, keepdims=True)
        shifted = jnp.exp(scores - peak)
        total = jnp.sum(shifted, axis=1, keepdims=True)
        weights = (shifted * (1.0 / total)).astype(jnp.bfloat16)
        outs.append(dot_nn(weights, v_ref[...]))
        norms.append(peak + jnp.log(total))
    lanes = lax.broadcasted_iota(jnp.int32, out_ref.shape, 1)
    out_ref[...] = jnp.where(lanes < 64, outs[0], outs[1]).astype(jnp.bfloat16)
    lse_ref[...] = jnp.where(lanes < 64, norms[0], norms[1])


def backward_kernel(
    q_ref, k_ref, v_ref, g_ref, seg_col, seg_row, vec_ref, lse_ref,
    dq_ref, dk_ref, dv_ref, diag_ref, far_ref, strip, sums, dk_sum, dv_sum,
):
    length = k_ref.shape[0]
    block = pl.program_id(1)
    left = length - ROWS - NEAR

    @pl.when(block == 0)
    def _():
        fill_strip(strip, vec_ref, length)
        sums[...] = jnp.zeros_like(sums)
        dk_sum[...] = jnp.zeros_like(dk_sum)
        dv_sum[...] = jnp.zeros_like(dv_sum)

    start = pl.multiple_of(length - ROWS - block * ROWS, ROWS)
    same_doc = seg_col[...] == seg_row[...]
    queries_grad = []
    for head in range(2):
        query = head_lanes(q_ref[...], head)
        out_grad = head_lanes(g_ref[...], head)
        scores = dot_nt(query, k_ref[...]) * 0.125
        scores = scores + strip[head, :, pl.ds(start, length)]
        norm = lse_ref[:, 64 * head : 64 * head + 1]
        probs = jnp.where(same_doc, jnp.exp(scores - norm), 0.0)
        grad_probs = dot_nt(out_grad, v_ref[...])
        row_dot = jnp.sum(probs * grad_probs, axis=1, keepdims=True)
        grad_scores = probs * (grad_probs - row_dot)
        sums[head, :, pl.ds(start, length)] += grad_scores
        low_scores = grad_scores.astype(jnp.bfloat16)
        queries_grad.append(dot_nn(low_scores, k_ref[...]))
        dk_sum[...] += dot_tn(low_scores, query)
        dv_sum[...] += dot_tn(probs.astype(jnp.bfloat16), out_grad)
    lanes = lax.broadcasted_iota(jnp.int32, dq_ref.shape, 1)
    joined = jnp.where(lanes < 64, queries_grad[0], queries_grad[1]) * 0.125
    dq_ref[...] = joined.astype(jnp.bfloat16)

    @pl.when(block == pl.num_programs(1) - 1)
    def _():
        dk_ref[...] = (dk_sum[...] * 0.125).astype(jnp.bfloat16)
        dv_ref[...] = dv_sum[...].astype(jnp.bfloat16)
        for head in range(2):
            near = sums[head, :, left : left + SPAN]
            lanes = lax.broadcasted_iota(jnp.int32, near.shape, 1)
            rows = lax.broadcasted_iota(jnp.int32, near.shape, 0)
            relative = lanes - rows - NEAR
            low = jnp.sum(jnp.where(relative <= -NEAR, near, 0.0), axis=0, keepdims=True)
            high = jnp.sum(jnp.where(relative >= NEAR, near, 0.0), axis=0, keepdims=True)
            inside = jnp.where(jnp.abs(relative) < NEAR, near, 0.0)
            diag_ref[0, head : head + 1, :] = jnp.sum(skew(inside, False), axis=0, keepdims=True)
            low_total = jnp.sum(low) + jnp.sum(sums[head, :, :left])
            high_total = jnp.sum(high) + jnp.sum(sums[head, :, left + SPAN :])
            side = lax.broadcasted_iota(jnp.int32, (1, 128), 1)
            far_ref[0, head : head + 1, :] = jnp.where(side < 64, low_total, high_total)


def attention_specs(length, pairs):
    whole = lambda part: pl.BlockSpec((length, 128), lambda p, b: (0, part * pairs + p))
    rows = pl.BlockSpec((ROWS, 128), lambda p, b: (b, p))
    seg_col = pl.BlockSpec((ROWS, 1), lambda p, b: (b, 0))
    seg_row = pl.BlockSpec((1, length), lambda p, b: (0, 0))
    vec = pl.BlockSpec((1, 2, SPAN), lambda p, b: (p, 0, 0))
    return whole, rows, seg_col, seg_row, vec


def attention_forward(packed, segment_row, bias_vec):
    length = packed.shape[0]
    pairs = packed.shape[1] // (3 * 128)
    whole, rows, seg_col, seg_row, vec = attention_specs(length, pairs)
    return pl.pallas_call(
        forward_kernel,
        grid=(pairs, length // ROWS),
        in_specs=[rows, whole(1), whole(2), seg_col, seg_row, vec],
        out_specs=[rows, rows],
        out_shape=[
            jax.ShapeDtypeStruct((length, pairs * 128), jnp.bfloat16),
            jax.ShapeDtypeStruct((length, pairs * 128), jnp.float32),
        ],
        scratch_shapes=[pltpu.VMEM((2, ROWS, 2 * length - ROWS), jnp.float32)],
        compiler_params=pltpu.CompilerParams(vmem_limit_bytes=40 * 1024 * 1024),
        cost_estimate=pl.CostEstimate(
            flops=pairs * 2 * 2 * 2 * length * length * 128,
            bytes_accessed=4 * pairs * length * 128 * 2,
            transcendentals=pairs * 2 * length * length,
        ),
        name="attention_forward",
    )(packed, packed, packed, segment_row[:, None], segment_row[None, :], bias_vec)


def attention_backward(packed, out_grad, segment_row, bias_vec, log_norm):
    length = packed.shape[0]
    pairs = packed.shape[1] // (3 * 128)
    whole, rows, seg_col, seg_row, vec = attention_specs(length, pairs)
    low = jax.ShapeDtypeStruct((length, pairs * 128), jnp.bfloat16)
    return pl.pallas_call(
        backward_kernel,
        grid=(pairs, length // ROWS),
        in_specs=[rows, whole(1), whole(2), rows, seg_col, seg_row, vec, rows],
        out_specs=[
            rows,
            whole(0),
            whole(0),
            vec,
            pl.BlockSpec((1, 2, 128), lambda p, b: (p, 0, 0)),
        ],
        out_shape=[
            low,
            low,
            low,
            jax.ShapeDtypeStruct((pairs, 2, SPAN), jnp.float32),
            jax.ShapeDtypeStruct((pairs, 2, 128), jnp.float32),
        ],
        scratch_shapes=[
            pltpu.VMEM((2, ROWS, 2 * length - ROWS), jnp.float32),
            pltpu.VMEM((2, ROWS, 2 * length - ROWS), jnp.float32),
            pltpu.VMEM((length, 128), jnp.float32),
            pltpu.VMEM((length, 128), jnp.float32),
        ],
        compiler_params=pltpu.CompilerParams(vmem_limit_bytes=48 * 1024 * 1024),
        cost_estimate=pl.CostEstimate(
            flops=pairs * 2 * 5 * 2 * length * length * 128,
            bytes_accessed=9 * pairs * length * 128 * 2,
            transcendentals=pairs * 2 * length * length,
        ),
        name="attention_backward",
    )(packed, packed, packed, out_grad, segment_row[:, None], segment_row[None, :], bias_vec, log_norm)


def gelu_tanh(inner_act):
    return jax.nn.gelu(inner_act, approximate=True)


def swap(values):
    return lax.ppermute(values, "tensor", [(0, 1), (1, 0)])


def heads_total(partial_sum):
    return partial_sum + swap(partial_sum)


def exchange(rows, model_width):
    grouped = rows.reshape(lax.axis_size("dp"), -1, model_width)
    return lax.all_to_all(grouped, "dp", split_axis=0, concat_axis=0, tiled=True)


def to_owners(rows, model_width):
    arrived = exchange(rows, model_width)
    return jnp.concatenate([arrived, swap(arrived)], axis=0)


def to_senders(partial_rows, model_width):
    kept, given = jnp.split(partial_rows.reshape(2, -1, model_width), 2, axis=0)
    summed = kept + swap(given.astype(jnp.bfloat16)).astype(jnp.float32)
    arrived = exchange(summed.astype(jnp.bfloat16), model_width).reshape(-1, model_width)
    return jnp.concatenate([arrived, swap(arrived)], axis=0)


def all_to_all(shares):
    return lax.all_to_all(shares, "dp", split_axis=0, concat_axis=0, tiled=True)


def scatter_rows(values):
    return values.reshape((lax.axis_size("dp"), -1) + values.shape[1:]).astype(jnp.bfloat16)


def to_everyone(rows):
    return jnp.broadcast_to(rows[None], (lax.axis_size("dp"),) + rows.shape).astype(jnp.bfloat16)


def per_device(
    tokens,
    segments,
    gain_attn,
    w_qkv,
    w_attn_out,
    bias_table,
    gain_ffn,
    router,
    expert_in,
    expert_out,
    expert_ids,
    cotangent,
):
    length, model_width = tokens.shape
    head_cols = w_qkv.shape[2]
    heads_here = bias_table.shape[1]
    head_size = head_cols // heads_here
    experts_all = router.shape[1]
    experts_here = expert_in.shape[0]
    capacity = max(2, 2 * length // experts_all)
    half = capacity // 2
    segment_row = segments[0]
    bucket_count = bias_table.shape[0]
    near_hot = (
        near_buckets(bucket_count)[:, None] == jnp.arange(bucket_count, dtype=jnp.int32)[None, :]
    ).astype(jnp.float32)
    bias_vec = jnp.sum(near_hot[None] * bias_table.T[:, None, :], axis=2)
    bias_vec = bias_vec.reshape(heads_here // 2, 2, SPAN)
    chosen = expert_ids[:, 0]
    one_hot_int = (chosen[:, None] == jnp.arange(experts_all, dtype=jnp.int32)[None, :]).astype(
        jnp.int32
    )
    one_hot_float = one_hot_int.astype(jnp.float32)
    earlier = jnp.arange(length)[None, :] < jnp.arange(length)[:, None]
    ranks = jnp.dot(
        earlier.astype(jnp.bfloat16),
        one_hot_float.astype(jnp.bfloat16),
        preferred_element_type=jnp.float32,
    )
    slot_ids = jnp.sum(ranks * one_hot_float, axis=1).astype(jnp.int32)
    side = (slot_ids >= half).astype(jnp.int32)
    other_side = (side != lax.axis_index("tensor")).astype(jnp.int32)
    target_rows = chosen * half + slot_ids - side * half + other_side * (experts_all * half)
    own_slots = jnp.arange(experts_all * half, dtype=jnp.int32)
    place = (own_slots[:, None] == target_rows[None, :]).astype(jnp.bfloat16)
    all_slots = jnp.arange(2 * experts_all * half, dtype=jnp.int32)
    pick = (target_rows[:, None] == all_slots[None, :]).astype(jnp.bfloat16)
    upstream = cotangent.astype(jnp.float32)
    cotangent_sent = jnp.dot(place, cotangent, preferred_element_type=jnp.float32)
    cotangent_rows = to_owners(cotangent_sent.astype(jnp.bfloat16), model_width)
    inputs32 = tokens.astype(jnp.float32)
    scale_one = lax.rsqrt(jnp.mean(inputs32 * inputs32, axis=1, keepdims=True) + epsilon)
    normed_one = inputs32 * scale_one
    normed = (normed_one * gain_attn).astype(jnp.bfloat16)
    w_flat = w_qkv.reshape(model_width, 3 * head_cols)
    packed = jnp.dot(normed, w_flat, preferred_element_type=jnp.float32).astype(jnp.bfloat16)
    mixed_heads, log_norm = attention_forward(packed, segment_row, bias_vec)
    attn_part = jnp.dot(mixed_heads, w_attn_out, preferred_element_type=jnp.float32)
    hidden = inputs32 + heads_total(attn_part)
    scale_two = lax.rsqrt(jnp.mean(hidden * hidden, axis=1, keepdims=True) + epsilon)
    normed_two = hidden * scale_two
    ffn_in = normed_two * gain_ffn
    router_logits = jnp.dot(ffn_in, router, precision=highest)
    logit_peak = jnp.max(router_logits, axis=1, keepdims=True)
    router_exp = jnp.exp(router_logits - logit_peak)
    router_probs = router_exp / jnp.sum(router_exp, axis=1, keepdims=True)
    gate_prob = jnp.sum(router_probs * one_hot_float, axis=1)
    gate_high = lax.reduce_precision(gate_prob, 8, 7)
    gate_mid = lax.reduce_precision(gate_prob - gate_high, 8, 7)
    gate_low = gate_prob - gate_high - gate_mid
    gate_parts = jnp.stack([gate_high, gate_mid, gate_low], axis=1)
    gate_parts = jnp.pad(gate_parts, ((0, 0), (0, 125))).astype(jnp.bfloat16)
    sent = jnp.concatenate([ffn_in.astype(jnp.bfloat16), gate_parts], axis=1)
    send_rows = jnp.dot(place, sent, preferred_element_type=jnp.float32)
    arrived_rows = to_owners(send_rows.astype(jnp.bfloat16), model_width + 128)
    expert_rows = arrived_rows[:, :, :model_width].reshape(-1, experts_here, half, model_width)
    gate_rows = jnp.sum(
        arrived_rows[:, :, model_width:].astype(jnp.float32), axis=2, keepdims=True
    )
    expert_grads = (gate_rows * cotangent_rows.astype(jnp.float32)).astype(jnp.bfloat16)
    expert_grads = expert_grads.reshape(-1, experts_here, half, model_width)
    inner_act = jnp.einsum(
        "secd,edf->secf", expert_rows, expert_in, preferred_element_type=jnp.float32
    )
    activated, gelu_back = jax.vjp(gelu_tanh, inner_act)
    act_low = activated.astype(jnp.bfloat16)
    expert_part = jnp.einsum(
        "secf,efd->secd", act_low, expert_out, preferred_element_type=jnp.float32
    )
    returned = to_senders(expert_part, model_width)
    picked = jnp.dot(pick, returned, preferred_element_type=jnp.float32)
    output = (hidden + gate_prob[:, None] * picked).astype(jnp.bfloat16)
    grad_gate = jnp.sum(upstream * picked, axis=1)
    grad_act = jnp.einsum(
        "secd,efd->secf", expert_grads, expert_out, preferred_element_type=jnp.float32
    )
    grad_inner = gelu_back(grad_act)[0].astype(jnp.bfloat16)
    grad_rows = jnp.einsum(
        "secf,edf->secd", grad_inner, expert_in, preferred_element_type=jnp.float32
    )
    grad_sent = jnp.dot(
        pick, to_senders(grad_rows, model_width), preferred_element_type=jnp.float32
    )
    grad_logits = router_probs * (one_hot_float - gate_prob[:, None]) * grad_gate[:, None]
    grad_router = jnp.dot(ffn_in.T, grad_logits, precision=highest)
    grad_ffn_in = grad_sent + jnp.dot(grad_logits, router.T, precision=highest)
    grad_gain_ffn = jnp.sum(grad_ffn_in * normed_two, axis=0)
    grad_norm_two = grad_ffn_in * gain_ffn
    grad_hidden = upstream + scale_two * (
        grad_norm_two - normed_two * jnp.mean(grad_norm_two * normed_two, axis=1, keepdims=True)
    )
    grad_attn = grad_hidden.astype(jnp.bfloat16)
    grad_w_attn_out = jnp.dot(mixed_heads.T, grad_attn, preferred_element_type=jnp.float32)
    grad_mixed = jnp.dot(grad_attn, w_attn_out.T, preferred_element_type=jnp.float32).astype(
        jnp.bfloat16
    )
    share_rows = head_cols // lax.axis_size("dp")
    early_sent = jnp.concatenate(
        [
            scatter_rows(grad_w_attn_out),
            scatter_rows(grad_router.reshape(-1, model_width)),
            to_everyone(grad_gain_ffn[None]),
        ],
        axis=1,
    )
    early_share = jnp.sum(all_to_all(early_sent).astype(jnp.float32), axis=0)
    total_gain_ffn = early_share[-1]
    early_all = all_to_all(to_everyone(early_share[:-1])).astype(jnp.float32)
    total_attn_out = early_all[:, :share_rows].reshape(head_cols, model_width)
    total_router = early_all[:, share_rows:].reshape(router.shape)
    grad_queries, grad_keys, grad_values, diagonals, far = attention_backward(
        packed, grad_mixed, segment_row, bias_vec, log_norm
    )
    grad_table = jnp.sum(diagonals.reshape(heads_here, SPAN)[:, :, None] * near_hot[None], axis=1)
    far = far.reshape(heads_here, 128)
    half_count = bucket_count // 2
    bucket_row = jnp.arange(bucket_count, dtype=jnp.int32)[None, :]
    grad_table = grad_table + jnp.where(bucket_row == half_count - 1, far[:, :1], 0.0)
    grad_table = grad_table + jnp.where(bucket_row == bucket_count - 1, far[:, 127:], 0.0)
    grad_packed = jnp.concatenate([grad_queries, grad_keys, grad_values], axis=1)
    grad_packed, late_grads, late_rows = lax.optimization_barrier(
        (grad_packed, expert_grads, expert_rows)
    )
    grad_expert_out = jnp.einsum(
        "secf,secd->efd", act_low, late_grads, preferred_element_type=jnp.float32
    )
    grad_expert_in = jnp.einsum(
        "secd,secf->edf", late_rows, grad_inner, preferred_element_type=jnp.float32
    )
    grad_w_qkv = jnp.dot(normed.T, grad_packed, preferred_element_type=jnp.float32)
    grad_normed = heads_total(jnp.dot(grad_packed, w_flat.T, preferred_element_type=jnp.float32))
    grad_gain_attn = jnp.sum(grad_normed * normed_one, axis=0)
    grad_norm_one = grad_normed * gain_attn
    grad_tokens = grad_hidden + scale_one * (
        grad_norm_one - normed_one * jnp.mean(grad_norm_one * normed_one, axis=1, keepdims=True)
    )
    qkv_share = jnp.sum(all_to_all(scatter_rows(grad_w_qkv)).astype(jnp.float32), axis=0)
    small = jnp.concatenate([grad_gain_attn, grad_table.T.reshape(-1)])
    small = jnp.pad(small, (0, -small.shape[0] % (3 * head_cols))).reshape(-1, 3 * head_cols)
    late_all = all_to_all(to_everyone(jnp.concatenate([qkv_share, small], axis=0)))
    late_all = late_all.astype(jnp.float32)
    total_w_qkv = late_all[:, : qkv_share.shape[0]].reshape(w_qkv.shape)
    small_total = jnp.sum(late_all[:, qkv_share.shape[0] :], axis=0).reshape(-1)
    total_gain = small_total[:model_width]
    total_table = small_total[model_width : model_width + grad_table.size]
    total_table = total_table.reshape(bias_table.shape)
    return (
        output,
        grad_tokens,
        total_gain,
        total_w_qkv,
        total_attn_out,
        total_table,
        total_gain_ffn,
        total_router,
        grad_expert_in,
        grad_expert_out,
    )


def solution(mesh):
    return jax.shard_map(
        per_device,
        mesh=mesh,
        in_specs=(
            P("dp", None),
            P("dp", None),
            P(),
            P(None, None, "tensor"),
            P("tensor", None),
            P(None, "tensor"),
            P(),
            P(),
            P("dp", None, "tensor"),
            P("dp", "tensor", None),
            P("dp", None),
            P("dp", None),
        ),
        out_specs=(
            P("dp", None),
            P("dp", None),
            P(),
            P(None, None, "tensor"),
            P("tensor", None),
            P(None, "tensor"),
            P(),
            P(),
            P("dp", None, "tensor"),
            P("dp", "tensor", None),
        ),
        check_vma=False,
    )
```

```python
import jax
import jax.numpy as jnp
from jax import lax
from jax.experimental import pallas as pl
from jax.experimental.pallas import tpu as pltpu
from jax.sharding import PartitionSpec as P

epsilon = 1e-06
highest = lax.Precision.HIGHEST
bucket_edges = (8, 12, 16, 23, 32, 46, 64, 91)


def bucket_ids(row_positions, col_positions, half_count):
    offset = col_positions[None, :] - row_positions[:, None]
    distance = jnp.abs(offset)
    far_part = jnp.zeros_like(distance)
    for edge_value in bucket_edges:
        far_part = far_part + (distance >= edge_value).astype(jnp.int32)
    near_far = jnp.where(distance < 8, distance, 7 + far_part)
    return near_far + half_count * (offset > 0).astype(jnp.int32)


NEAR = 128
ROWS = 256
SPAN = ROWS + 2 * NEAR


def near_buckets(bucket_count):
    zero = jnp.zeros((1,), jnp.int32)
    relative = jnp.arange(SPAN, dtype=jnp.int32) - NEAR
    return bucket_ids(zero, relative, bucket_count // 2)[0]


def skew(values, right):
    rows = lax.broadcasted_iota(jnp.int32, values.shape, 0)
    width = values.shape[1]
    step = 1
    while step < values.shape[0]:
        rolled = pltpu.roll(values, step if right else width - step, 1)
        values = jnp.where((rows & step) != 0, rolled, values)
        step *= 2
    return values


def fill_strip(strip, vec_ref, length):
    left = length - ROWS - NEAR
    for head in range(2):
        row = vec_ref[0, head : head + 1, :]
        low = row[:, :1]
        high = row[:, SPAN - 1 :]
        spread = skew(jnp.broadcast_to(row, (ROWS, SPAN)), True)
        lanes = lax.broadcasted_iota(jnp.int32, (ROWS, SPAN), 1)
        rows = lax.broadcasted_iota(jnp.int32, (ROWS, SPAN), 0)
        strip[head, :, left : left + SPAN] = jnp.where(lanes < rows, low, spread)
        strip[head, :, :left] = jnp.broadcast_to(low, (ROWS, left))
        rest = strip.shape[2] - left - SPAN
        strip[head, :, left + SPAN :] = jnp.broadcast_to(high, (ROWS, rest))


def head_lanes(values, head):
    lanes = lax.broadcasted_iota(jnp.int32, values.shape, 1)
    keep = (lanes < 64) if head == 0 else (lanes >= 64)
    return jnp.where(keep, values, jnp.zeros_like(values))


def dot_nt(left, right):
    return lax.dot_general(left, right, (((1,), (1,)), ((), ())), preferred_element_type=jnp.float32)


def dot_tn(left, right):
    return lax.dot_general(left, right, (((0,), (0,)), ((), ())), preferred_element_type=jnp.float32)


def dot_nn(left, right):
    return jnp.dot(left, right, preferred_element_type=jnp.float32)


def forward_kernel(q_ref, k_ref, v_ref, seg_col, seg_row, vec_ref, out_ref, lse_ref, strip):
    length = k_ref.shape[0]
    block = pl.program_id(1)

    @pl.when(block == 0)
    def _():
        fill_strip(strip, vec_ref, length)

    start = pl.multiple_of(length - ROWS - block * ROWS, ROWS)
    same_doc = seg_col[...] == seg_row[...]
    outs = []
    norms = []
    for head in range(2):
        scores = dot_nt(head_lanes(q_ref[...], head), k_ref[...]) * 0.125
        scores = scores + strip[head, :, pl.ds(start, length)]
        scores = jnp.where(same_doc, scores, -1e30)
        peak = jnp.max(scores, axis=1, keepdims=True)
        shifted = jnp.exp(scores - peak)
        total = jnp.sum(shifted, axis=1, keepdims=True)
        weights = (shifted * (1.0 / total)).astype(jnp.bfloat16)
        outs.append(dot_nn(weights, v_ref[...]))
        norms.append(peak + jnp.log(total))
    lanes = lax.broadcasted_iota(jnp.int32, out_ref.shape, 1)
    out_ref[...] = jnp.where(lanes < 64, outs[0], outs[1]).astype(jnp.bfloat16)
    lse_ref[...] = jnp.where(lanes < 64, norms[0], norms[1])


def backward_kernel(
    q_ref, k_ref, v_ref, g_ref, seg_col, seg_row, vec_ref, lse_ref,
    dq_ref, dk_ref, dv_ref, diag_ref, far_ref, strip, sums, dk_sum, dv_sum,
):
    length = k_ref.shape[0]
    block = pl.program_id(1)
    left = length - ROWS - NEAR

    @pl.when(block == 0)
    def _():
        fill_strip(strip, vec_ref, length)
        sums[...] = jnp.zeros_like(sums)
        dk_sum[...] = jnp.zeros_like(dk_sum)
        dv_sum[...] = jnp.zeros_like(dv_sum)

    start = pl.multiple_of(length - ROWS - block * ROWS, ROWS)
    same_doc = seg_col[...] == seg_row[...]
    queries_grad = []
    for head in range(2):
        query = head_lanes(q_ref[...], head)
        out_grad = head_lanes(g_ref[...], head)
        scores = dot_nt(query, k_ref[...]) * 0.125
        scores = scores + strip[head, :, pl.ds(start, length)]
        norm = lse_ref[:, 64 * head : 64 * head + 1]
        probs = jnp.where(same_doc, jnp.exp(scores - norm), 0.0)
        grad_probs = dot_nt(out_grad, v_ref[...])
        row_dot = jnp.sum(probs * grad_probs, axis=1, keepdims=True)
        grad_scores = probs * (grad_probs - row_dot)
        sums[head, :, pl.ds(start, length)] += grad_scores
        low_scores = grad_scores.astype(jnp.bfloat16)
        queries_grad.append(dot_nn(low_scores, k_ref[...]))
        dk_sum[...] += dot_tn(low_scores, query)
        dv_sum[...] += dot_tn(probs.astype(jnp.bfloat16), out_grad)
    lanes = lax.broadcasted_iota(jnp.int32, dq_ref.shape, 1)
    joined = jnp.where(lanes < 64, queries_grad[0], queries_grad[1]) * 0.125
    dq_ref[...] = joined.astype(jnp.bfloat16)

    @pl.when(block == pl.num_programs(1) - 1)
    def _():
        dk_ref[...] = (dk_sum[...] * 0.125).astype(jnp.bfloat16)
        dv_ref[...] = dv_sum[...].astype(jnp.bfloat16)
        for head in range(2):
            near = sums[head, :, left : left + SPAN]
            lanes = lax.broadcasted_iota(jnp.int32, near.shape, 1)
            rows = lax.broadcasted_iota(jnp.int32, near.shape, 0)
            relative = lanes - rows - NEAR
            low = jnp.sum(jnp.where(relative <= -NEAR, near, 0.0), axis=0, keepdims=True)
            high = jnp.sum(jnp.where(relative >= NEAR, near, 0.0), axis=0, keepdims=True)
            inside = jnp.where(jnp.abs(relative) < NEAR, near, 0.0)
            diag_ref[0, head : head + 1, :] = jnp.sum(skew(inside, False), axis=0, keepdims=True)
            low_total = jnp.sum(low) + jnp.sum(sums[head, :, :left])
            high_total = jnp.sum(high) + jnp.sum(sums[head, :, left + SPAN :])
            side = lax.broadcasted_iota(jnp.int32, (1, 128), 1)
            far_ref[0, head : head + 1, :] = jnp.where(side < 64, low_total, high_total)


def attention_specs(length, pairs):
    whole = lambda part: pl.BlockSpec((length, 128), lambda p, b: (0, part * pairs + p))
    rows = pl.BlockSpec((ROWS, 128), lambda p, b: (b, p))
    seg_col = pl.BlockSpec((ROWS, 1), lambda p, b: (b, 0))
    seg_row = pl.BlockSpec((1, length), lambda p, b: (0, 0))
    vec = pl.BlockSpec((1, 2, SPAN), lambda p, b: (p, 0, 0))
    return whole, rows, seg_col, seg_row, vec


def attention_forward(packed, segment_row, bias_vec):
    length = packed.shape[0]
    pairs = packed.shape[1] // (3 * 128)
    whole, rows, seg_col, seg_row, vec = attention_specs(length, pairs)
    return pl.pallas_call(
        forward_kernel,
        grid=(pairs, length // ROWS),
        in_specs=[rows, whole(1), whole(2), seg_col, seg_row, vec],
        out_specs=[rows, rows],
        out_shape=[
            jax.ShapeDtypeStruct((length, pairs * 128), jnp.bfloat16),
            jax.ShapeDtypeStruct((length, pairs * 128), jnp.float32),
        ],
        scratch_shapes=[pltpu.VMEM((2, ROWS, 2 * length - ROWS), jnp.float32)],
        compiler_params=pltpu.CompilerParams(vmem_limit_bytes=40 * 1024 * 1024),
        cost_estimate=pl.CostEstimate(
            flops=pairs * 2 * 2 * 2 * length * length * 128,
            bytes_accessed=4 * pairs * length * 128 * 2,
            transcendentals=pairs * 2 * length * length,
        ),
        name="attention_forward",
    )(packed, packed, packed, segment_row[:, None], segment_row[None, :], bias_vec)


def attention_backward(packed, out_grad, segment_row, bias_vec, log_norm):
    length = packed.shape[0]
    pairs = packed.shape[1] // (3 * 128)
    whole, rows, seg_col, seg_row, vec = attention_specs(length, pairs)
    low = jax.ShapeDtypeStruct((length, pairs * 128), jnp.bfloat16)
    return pl.pallas_call(
        backward_kernel,
        grid=(pairs, length // ROWS),
        in_specs=[rows, whole(1), whole(2), rows, seg_col, seg_row, vec, rows],
        out_specs=[
            rows,
            whole(0),
            whole(0),
            vec,
            pl.BlockSpec((1, 2, 128), lambda p, b: (p, 0, 0)),
        ],
        out_shape=[
            low,
            low,
            low,
            jax.ShapeDtypeStruct((pairs, 2, SPAN), jnp.float32),
            jax.ShapeDtypeStruct((pairs, 2, 128), jnp.float32),
        ],
        scratch_shapes=[
            pltpu.VMEM((2, ROWS, 2 * length - ROWS), jnp.float32),
            pltpu.VMEM((2, ROWS, 2 * length - ROWS), jnp.float32),
            pltpu.VMEM((length, 128), jnp.float32),
            pltpu.VMEM((length, 128), jnp.float32),
        ],
        compiler_params=pltpu.CompilerParams(vmem_limit_bytes=48 * 1024 * 1024),
        cost_estimate=pl.CostEstimate(
            flops=pairs * 2 * 5 * 2 * length * length * 128,
            bytes_accessed=9 * pairs * length * 128 * 2,
            transcendentals=pairs * 2 * length * length,
        ),
        name="attention_backward",
    )(packed, packed, packed, out_grad, segment_row[:, None], segment_row[None, :], bias_vec, log_norm)


def gelu_tanh(inner_act):
    return jax.nn.gelu(inner_act, approximate=True)


def swap(values):
    return lax.ppermute(values, "tensor", [(0, 1), (1, 0)])


def heads_total(partial_sum):
    return partial_sum + swap(partial_sum)


def exchange(rows, model_width):
    grouped = rows.reshape(lax.axis_size("dp"), -1, model_width)
    return lax.all_to_all(grouped, "dp", split_axis=0, concat_axis=0, tiled=True)


def to_owners(rows, model_width):
    arrived = exchange(rows, model_width)
    return jnp.concatenate([arrived, swap(arrived)], axis=0)


def to_senders(partial_rows, model_width):
    kept, given = jnp.split(partial_rows.reshape(2, -1, model_width), 2, axis=0)
    summed = kept + swap(given.astype(jnp.bfloat16)).astype(jnp.float32)
    arrived = exchange(summed.astype(jnp.bfloat16), model_width).reshape(-1, model_width)
    return jnp.concatenate([arrived, swap(arrived)], axis=0)


def all_to_all(shares):
    return lax.all_to_all(shares, "dp", split_axis=0, concat_axis=0, tiled=True)


def scatter_rows(values):
    return values.reshape((lax.axis_size("dp"), -1) + values.shape[1:]).astype(jnp.bfloat16)


def to_everyone(rows):
    return jnp.broadcast_to(rows[None], (lax.axis_size("dp"),) + rows.shape).astype(jnp.bfloat16)


def per_device(
    tokens,
    segments,
    gain_attn,
    w_qkv,
    w_attn_out,
    bias_table,
    gain_ffn,
    router,
    expert_in,
    expert_out,
    expert_ids,
    cotangent,
):
    length, model_width = tokens.shape
    head_cols = w_qkv.shape[2]
    heads_here = bias_table.shape[1]
    head_size = head_cols // heads_here
    experts_all = router.shape[1]
    experts_here = expert_in.shape[0]
    capacity = max(2, 2 * length // experts_all)
    half = capacity // 2
    segment_row = segments[0]
    bucket_count = bias_table.shape[0]
    near_hot = (
        near_buckets(bucket_count)[:, None] == jnp.arange(bucket_count, dtype=jnp.int32)[None, :]
    ).astype(jnp.float32)
    bias_vec = jnp.sum(near_hot[None] * bias_table.T[:, None, :], axis=2)
    bias_vec = bias_vec.reshape(heads_here // 2, 2, SPAN)
    chosen = expert_ids[:, 0]
    one_hot_int = (chosen[:, None] == jnp.arange(experts_all, dtype=jnp.int32)[None, :]).astype(
        jnp.int32
    )
    one_hot_float = one_hot_int.astype(jnp.float32)
    earlier = jnp.arange(length)[None, :] < jnp.arange(length)[:, None]
    ranks = jnp.dot(
        earlier.astype(jnp.bfloat16),
        one_hot_float.astype(jnp.bfloat16),
        preferred_element_type=jnp.float32,
    )
    slot_ids = jnp.sum(ranks * one_hot_float, axis=1).astype(jnp.int32)
    side = (slot_ids >= half).astype(jnp.int32)
    other_side = (side != lax.axis_index("tensor")).astype(jnp.int32)
    target_rows = chosen * half + slot_ids - side * half + other_side * (experts_all * half)
    own_slots = jnp.arange(experts_all * half, dtype=jnp.int32)
    place = (own_slots[:, None] == target_rows[None, :]).astype(jnp.bfloat16)
    all_slots = jnp.arange(2 * experts_all * half, dtype=jnp.int32)
    pick = (target_rows[:, None] == all_slots[None, :]).astype(jnp.bfloat16)
    upstream = cotangent.astype(jnp.float32)
    cotangent_sent = jnp.dot(place, cotangent, preferred_element_type=jnp.float32)
    cotangent_arrived = exchange(cotangent_sent.astype(jnp.bfloat16), model_width)
    inputs32 = tokens.astype(jnp.float32)
    scale_one = lax.rsqrt(jnp.mean(inputs32 * inputs32, axis=1, keepdims=True) + epsilon)
    normed_one = inputs32 * scale_one
    normed = (normed_one * gain_attn).astype(jnp.bfloat16)
    w_flat = w_qkv.reshape(model_width, 3 * head_cols)
    packed = jnp.dot(normed, w_flat, preferred_element_type=jnp.float32).astype(jnp.bfloat16)
    mixed_heads, log_norm = attention_forward(packed, segment_row, bias_vec)
    mixed_heads, cotangent_arrived = lax.optimization_barrier((mixed_heads, cotangent_arrived))
    cotangent_rows = jnp.concatenate([cotangent_arrived, swap(cotangent_arrived)], axis=0)
    attn_part = jnp.dot(mixed_heads, w_attn_out, preferred_element_type=jnp.float32)
    hidden = inputs32 + heads_total(attn_part)
    scale_two = lax.rsqrt(jnp.mean(hidden * hidden, axis=1, keepdims=True) + epsilon)
    normed_two = hidden * scale_two
    ffn_in = normed_two * gain_ffn
    router_logits = jnp.dot(ffn_in, router, precision=highest)
    logit_peak = jnp.max(router_logits, axis=1, keepdims=True)
    router_exp = jnp.exp(router_logits - logit_peak)
    router_probs = router_exp / jnp.sum(router_exp, axis=1, keepdims=True)
    gate_prob = jnp.sum(router_probs * one_hot_float, axis=1)
    gate_high = lax.reduce_precision(gate_prob, 8, 7)
    gate_mid = lax.reduce_precision(gate_prob - gate_high, 8, 7)
    gate_low = gate_prob - gate_high - gate_mid
    gate_parts = jnp.stack([gate_high, gate_mid, gate_low], axis=1)
    gate_parts = jnp.pad(gate_parts, ((0, 0), (0, 125))).astype(jnp.bfloat16)
    sent = jnp.concatenate([ffn_in.astype(jnp.bfloat16), gate_parts], axis=1)
    send_rows = jnp.dot(place, sent, preferred_element_type=jnp.float32)
    arrived_rows = to_owners(send_rows.astype(jnp.bfloat16), model_width + 128)
    expert_rows = arrived_rows[:, :, :model_width].reshape(-1, experts_here, half, model_width)
    gate_rows = jnp.sum(
        arrived_rows[:, :, model_width:].astype(jnp.float32), axis=2, keepdims=True
    )
    expert_grads = (gate_rows * cotangent_rows.astype(jnp.float32)).astype(jnp.bfloat16)
    expert_grads = expert_grads.reshape(-1, experts_here, half, model_width)
    inner_act = jnp.einsum(
        "secd,edf->secf", expert_rows, expert_in, preferred_element_type=jnp.float32
    )
    activated, gelu_back = jax.vjp(gelu_tanh, inner_act)
    act_low = activated.astype(jnp.bfloat16)
    expert_part = jnp.einsum(
        "secf,efd->secd", act_low, expert_out, preferred_element_type=jnp.float32
    )
    returned = to_senders(expert_part, model_width)
    picked = jnp.dot(pick, returned, preferred_element_type=jnp.float32)
    output = (hidden + gate_prob[:, None] * picked).astype(jnp.bfloat16)
    grad_gate = jnp.sum(upstream * picked, axis=1)
    grad_act = jnp.einsum(
        "secd,efd->secf", expert_grads, expert_out, preferred_element_type=jnp.float32
    )
    grad_inner = gelu_back(grad_act)[0].astype(jnp.bfloat16)
    grad_rows = jnp.einsum(
        "secf,edf->secd", grad_inner, expert_in, preferred_element_type=jnp.float32
    )
    grad_sent = jnp.dot(
        pick, to_senders(grad_rows, model_width), preferred_element_type=jnp.float32
    )
    grad_logits = router_probs * (one_hot_float - gate_prob[:, None]) * grad_gate[:, None]
    grad_router = jnp.dot(ffn_in.T, grad_logits, precision=highest)
    grad_ffn_in = grad_sent + jnp.dot(grad_logits, router.T, precision=highest)
    grad_gain_ffn = jnp.sum(grad_ffn_in * normed_two, axis=0)
    grad_norm_two = grad_ffn_in * gain_ffn
    grad_hidden = upstream + scale_two * (
        grad_norm_two - normed_two * jnp.mean(grad_norm_two * normed_two, axis=1, keepdims=True)
    )
    grad_attn = grad_hidden.astype(jnp.bfloat16)
    grad_w_attn_out = jnp.dot(mixed_heads.T, grad_attn, preferred_element_type=jnp.float32)
    grad_mixed = jnp.dot(grad_attn, w_attn_out.T, preferred_element_type=jnp.float32).astype(
        jnp.bfloat16
    )
    share_rows = head_cols // lax.axis_size("dp")
    early_sent = jnp.concatenate(
        [
            scatter_rows(grad_w_attn_out),
            scatter_rows(grad_router.reshape(-1, model_width)),
            to_everyone(grad_gain_ffn[None]),
        ],
        axis=1,
    )
    early_share = jnp.sum(all_to_all(early_sent).astype(jnp.float32), axis=0)
    total_gain_ffn = early_share[-1]
    early_flat = early_share[:-1].reshape(-1)
    early_size = early_flat.shape[0]
    early_flat = jnp.pad(early_flat, (0, -early_size % (3 * head_cols)))
    early_rows = early_flat.reshape(-1, 3 * head_cols)
    grad_queries, grad_keys, grad_values, diagonals, far = attention_backward(
        packed, grad_mixed, segment_row, bias_vec, log_norm
    )
    grad_table = jnp.sum(diagonals.reshape(heads_here, SPAN)[:, :, None] * near_hot[None], axis=1)
    far = far.reshape(heads_here, 128)
    half_count = bucket_count // 2
    bucket_row = jnp.arange(bucket_count, dtype=jnp.int32)[None, :]
    grad_table = grad_table + jnp.where(bucket_row == half_count - 1, far[:, :1], 0.0)
    grad_table = grad_table + jnp.where(bucket_row == bucket_count - 1, far[:, 127:], 0.0)
    grad_packed = jnp.concatenate([grad_queries, grad_keys, grad_values], axis=1)
    grad_packed, late_grads, late_rows = lax.optimization_barrier(
        (grad_packed, expert_grads, expert_rows)
    )
    grad_expert_out = jnp.einsum(
        "secf,secd->efd", act_low, late_grads, preferred_element_type=jnp.float32
    )
    grad_expert_in = jnp.einsum(
        "secd,secf->edf", late_rows, grad_inner, preferred_element_type=jnp.float32
    )
    grad_w_qkv = jnp.dot(normed.T, grad_packed, preferred_element_type=jnp.float32)
    grad_normed = heads_total(jnp.dot(grad_packed, w_flat.T, preferred_element_type=jnp.float32))
    grad_gain_attn = jnp.sum(grad_normed * normed_one, axis=0)
    grad_norm_one = grad_normed * gain_attn
    grad_tokens = grad_hidden + scale_one * (
        grad_norm_one - normed_one * jnp.mean(grad_norm_one * normed_one, axis=1, keepdims=True)
    )
    qkv_sent = scatter_rows(grad_w_qkv)
    qkv_rows = qkv_sent.shape[1]
    late_sent = jnp.concatenate([qkv_sent, to_everyone(early_rows)], axis=1)
    late_arrived = all_to_all(late_sent)
    qkv_share = jnp.sum(late_arrived[:, :qkv_rows].astype(jnp.float32), axis=0)
    early_all = late_arrived[:, qkv_rows:].reshape(late_arrived.shape[0], -1)[:, :early_size]
    early_all = early_all.reshape(-1, share_rows + 1, model_width).astype(jnp.float32)
    total_attn_out = early_all[:, :share_rows].reshape(head_cols, model_width)
    total_router = early_all[:, share_rows:].reshape(router.shape)
    small = jnp.concatenate([grad_gain_attn, grad_table.T.reshape(-1)])
    small = jnp.pad(small, (0, -small.shape[0] % (3 * head_cols))).reshape(-1, 3 * head_cols)
    late_all = all_to_all(to_everyone(jnp.concatenate([qkv_share, small], axis=0)))
    qkv_parts = [
        late_all[:, :qkv_rows, part * head_cols : (part + 1) * head_cols].reshape(
            model_width, head_cols
        )
        for part in range(3)
    ]
    total_w_qkv = jnp.stack(qkv_parts, axis=1).astype(jnp.float32)
    small_total = jnp.sum(late_all[:, qkv_rows:].astype(jnp.float32), axis=0).reshape(-1)
    total_gain = small_total[:model_width]
    total_table = small_total[model_width : model_width + grad_table.size]
    total_table = total_table.reshape(bias_table.shape)
    return (
        output,
        grad_tokens,
        total_gain,
        total_w_qkv,
        total_attn_out,
        total_table,
        total_gain_ffn,
        total_router,
        grad_expert_in,
        grad_expert_out,
    )


def solution(mesh):
    return jax.shard_map(
        per_device,
        mesh=mesh,
        in_specs=(
            P("dp", None),
            P("dp", None),
            P(),
            P(None, None, "tensor"),
            P("tensor", None),
            P(None, "tensor"),
            P(),
            P(),
            P("dp", None, "tensor"),
            P("dp", "tensor", None),
            P("dp", None),
            P("dp", None),
        ),
        out_specs=(
            P("dp", None),
            P("dp", None),
            P(),
            P(None, None, "tensor"),
            P("tensor", None),
            P(None, "tensor"),
            P(),
            P(),
            P("dp", None, "tensor"),
            P("dp", "tensor", None),
        ),
        check_vma=False,
    )
```
